32 devices in a mesh: rep: 8 (over z, x), seq: 4 (over y, core).
Axes of the slice: x: 2, y: 2, z: 4, core: 2. Of those that a mesh axis runs over, the one named last changes fastest.
Arguments:
- tokens: bfloat16 [8, 1024, 6144], P('rep', 'seq'), may hold values from -6 to 6
- queries: bfloat16 [8, 1024, 128], P('rep', 'seq'), may hold values from -4 to 4
- ctx_grad: bfloat16 [8, 1024, 128], P('rep', 'seq'), may hold values from -0.5 to 0.5
- kv_weight: bfloat16 [8, 6144, 256], P('rep', 'seq'), may hold values from -0.078125 to 0.078125
- rand_blocks: int32 [16, 3], replicated, may hold values from 0 to 15
- step_count: int32 [1], replicated, may hold values from 0 to 63
Outputs:
- mixed_update: float32 [8, 6144, 256], P('rep', 'seq')
- query_grad: bfloat16 [8, 1024, 128], P('rep', 'seq')
The draws below stay inside these ranges and needn't reach their ends.
Inputs may be any that keep to these rules, and one draw needn't show every extreme that they name: `rand_blocks`: block indices of the same replica sequence.
All inputs are finite; a program needn't handle non-finite values.
Results may differ from the reference program's by a relative error of at most 0.02.
Values may be sent and summed in bfloat16 or wider, within the bound.
A program may use at most 64 MiB of HBM per device.

```python
import jax
import jax.numpy as jnp
from jax import lax

D = 6144
HD = 128
BLOCK = 64
RAND = 3
TOK_DEV = 256
TOKENS = 1024
NBLK = 16
N_REP = 8
N_SEQ = 4


def set_ends(result, stream_key, least, top_value):
    index_at = [jax.random.randint(jax.random.fold_in(stream_key, axis), (), 0, length) for axis, length in enumerate(result.shape)]
    longest = result.shape.index(max(result.shape))
    neighbour = index_at[:longest] + [(index_at[longest] + 1) % result.shape[longest]] + index_at[longest + 1:]
    return result.at[tuple(index_at)].set(least).at[tuple(neighbour)].set(top_value)


def block_scale(rng, dims, pieces, least, top_value):
    level, own = 1.0, jax.random.fold_in(rng, 6)
    for axis_at, shards_of in pieces:
        steps = jnp.exp(jax.random.uniform(jax.random.fold_in(own, axis_at), (shards_of,), jnp.float32, least / len(pieces), top_value / len(pieces)))
        level = level * jnp.repeat(steps, dims[axis_at] // shards_of).reshape([-1 if axis == axis_at else 1 for axis in range(len(dims))])
    return level


def bell_draw(stream_key, dims, deviation, bound, shards=(), kind=jnp.bfloat16):
    gain = block_scale(stream_key, dims, shards, -0.22, 0.18) if shards else 1.0
    entries = jax.random.normal(stream_key, dims, jnp.float32) * deviation * gain
    return jnp.minimum(jnp.maximum(entries, -bound), bound).astype(kind)


def setup_inputs(seed: int = 0) -> dict:
    splits = jax.random.split(jax.random.key(seed), 7)
    tokens = bell_draw(splits[0], (N_REP, TOKENS, D), 1.0, 6.0, ((0, 8), (1, 4)))
    queries = bell_draw(splits[1], (N_REP, TOKENS, HD), 0.5, 4.0, ((0, 8), (1, 4)))
    ctx_grad = bell_draw(splits[2], (N_REP, TOKENS, HD), (TOKENS ** -0.5), 0.5, ((0, 8), (1, 4)))
    kv_weight = bell_draw(splits[3], (N_REP, D, 2 * HD), D ** -0.5, 0.078125, ((0, 8), (1, 4)))
    rand_blocks = set_ends(jax.random.randint(splits[4], (NBLK, RAND), 0, NBLK), jax.random.fold_in(splits[4], 1), 0, NBLK - 1).astype(jnp.int32)
    step_count = jax.random.randint(splits[5], (1,), 0, 64).astype(jnp.int32)
    return {"tokens": tokens, "queries": queries, "ctx_grad": ctx_grad, "kv_weight": kv_weight, "rand_blocks": rand_blocks, "step_count": step_count}


def token_mask(rand_blocks):
    row_ids = jnp.arange(NBLK, dtype=jnp.int32)[:, None]
    col_ids = jnp.arange(NBLK, dtype=jnp.int32)[None, :]
    is_near = jnp.abs(row_ids - col_ids) <= 1
    picked = jnp.any(rand_blocks[:, :, None] == col_ids[:, None, :], axis=1)
    allowed = is_near | (col_ids == 0) | picked
    return jnp.repeat(jnp.repeat(allowed, BLOCK, axis=0), BLOCK, axis=1)


def one_replica(allowed, arrays):
    tok_rows, query_rows, grad_rows, weight_rows = arrays
    kv_rows = jnp.dot(tok_rows, weight_rows, preferred_element_type=jnp.float32).astype(jnp.bfloat16)
    keys_all = kv_rows[:, :HD]
    values_all = kv_rows[:, HD:]
    inv_root = HD ** -0.5
    scores = jnp.dot(query_rows, keys_all.T, preferred_element_type=jnp.float32) * inv_root
    unnorm = jnp.where(allowed, jnp.exp(scores), jnp.float32(0.0))
    row_total = jnp.sum(unnorm, axis=1, keepdims=True)
    prob_rows = unnorm / row_total
    prob_low = prob_rows.astype(jnp.bfloat16)
    context = jnp.dot(prob_low, values_all, preferred_element_type=jnp.float32)
    row_delta = jnp.sum(grad_rows.astype(jnp.float32) * context, axis=1, keepdims=True)
    prob_grad = jnp.dot(grad_rows, values_all.T, preferred_element_type=jnp.float32)
    score_grad = (prob_rows * (prob_grad - row_delta) * inv_root).astype(jnp.bfloat16)
    query_grad = jnp.dot(score_grad, keys_all, preferred_element_type=jnp.float32).astype(jnp.bfloat16)
    key_grad = jnp.dot(score_grad.T, query_rows, preferred_element_type=jnp.float32)
    value_grad = jnp.dot(prob_low.T, grad_rows, preferred_element_type=jnp.float32)
    kv_grad = jnp.concatenate([key_grad, value_grad], axis=1).astype(jnp.bfloat16)
    tok_split = tok_rows.reshape(N_SEQ, TOK_DEV, D)
    grad_split = kv_grad.reshape(N_SEQ, TOK_DEV, 2 * HD)

    def partial_sum(pair):
        return jnp.dot(pair[0].T, pair[1], preferred_element_type=jnp.float32).astype(jnp.bfloat16)

    partials = lax.map(partial_sum, (tok_split, grad_split))
    partials = lax.optimization_barrier(partials)
    weight_grad = jnp.sum(partials.astype(jnp.float32), axis=0)
    return weight_grad, query_grad


def reference(tokens, queries, ctx_grad, kv_weight, rand_blocks, step_count):
    allowed = token_mask(rand_blocks)
    weight_grad, query_grad = lax.map(lambda arrays: one_replica(allowed, arrays), (tokens, queries, ctx_grad, kv_weight))
    distance = jnp.left_shift(jnp.int32(1), step_count[0] % 4)
    mixed_update = (weight_grad + jnp.roll(weight_grad, distance, axis=0) + jnp.roll(weight_grad, -distance, axis=0)) / 3.0
    return mixed_update, query_grad
```

```python
from functools import partial

import jax
import jax.numpy as jnp
from jax import lax
from jax.experimental import pallas as pl
from jax.experimental.pallas import tpu as pltpu
from jax.sharding import PartitionSpec as P

BLOCK = 64
CHUNKS = 2
MESH = pl.DeviceIdType.MESH
BF16 = jnp.bfloat16
F32 = jnp.float32


def dot(a, b, dims):
    return lax.dot_general(a, b, (dims, ((), ())), preferred_element_type=F32)


def kernel(
    dist, rep_count, seq_count,
    tok_hbm, query, grad, weight, rand,
    mixed, query_grad,
    tok, wbuf, kvbuf, prob, terms_out, terms_in, kv_grad, acc,
    sib_out, sib_in, peer_out, peer_in, gossip_out, gossip_in, relay_out,
    local_sem, w_send, w_recv, fwd_send, fwd_recv, kv_send, kv_recv, term_send, term_recv,
    sib_send, sib_recv, peer_send, peer_recv, gos_send, gos_recv,
):
    n_tok = tok.shape[0]
    rows = wbuf.shape[2]
    head = wbuf.shape[3]
    part = rows // CHUNKS
    chips = seq_count // 2
    inv_root = head ** (-0.5)
    rep = lax.axis_index("rep")
    me = lax.axis_index("seq")
    chip, core = me // 2, me % 2
    sib = chip * 2 + (1 - core)
    sent = []

    def seq_other(step):
        return lax.rem(me + step, seq_count)

    def peer(step):
        return lax.rem(chip + step, chips) * 2 + core

    def peer_sib(step):
        return lax.rem(chip + step, chips) * 2 + (1 - core)

    def send(src, dst, send_sem, recv_sem, target):
        copy = pltpu.make_async_remote_copy(
            src_ref=src, dst_ref=dst, send_sem=send_sem, recv_sem=recv_sem,
            device_id=target, device_id_type=MESH,
        )
        copy.start()
        sent.append(copy)

    def arrived(ref, send_sem, recv_sem):
        pltpu.make_async_remote_copy(
            src_ref=ref, dst_ref=ref, send_sem=send_sem, recv_sem=recv_sem,
            device_id={"seq": sib}, device_id_type=MESH,
        ).wait_recv()

    two_step = dist == 1 and rep_count % 2 == 0 and rep_count > 2
    if dist == 0:
        partners = []
    elif two_step:
        side = rep % 2
        next_rep = lax.rem(rep + rep_count + 4 * side - 2, rep_count)
        prev_rep = lax.rem(rep + rep_count - 4 * side + 2, rep_count)
        pair_rep = rep + 1 - 2 * side
        partners = [next_rep, prev_rep, pair_rep] if rep_count > 4 else [next_rep, pair_rep]
    elif 2 * dist % rep_count == 0:
        partners = [lax.rem(rep + dist, rep_count)]
    else:
        partners = [lax.rem(rep + dist, rep_count), lax.rem(rep + rep_count - dist, rep_count)]

    tok_copy = pltpu.make_async_copy(tok_hbm.at[0], tok, local_sem.at[0])
    tok_copy.start()
    own_copies = []
    for half in range(2):
        copy = pltpu.make_async_copy(
            weight.at[0, :, pl.ds(half * head, head)], wbuf.at[half, me], local_sem.at[1 + half]
        )
        copy.start()
        own_copies.append(copy)

    barrier = pltpu.get_barrier_semaphore()
    for step in range(1, seq_count):
        pl.semaphore_signal(barrier, inc=1, device_id={"seq": seq_other(step)}, device_id_type=MESH)
    for partner in partners:
        pl.semaphore_signal(barrier, inc=1, device_id={"rep": partner}, device_id_type=MESH)
    pl.semaphore_wait(barrier, seq_count - 1 + len(partners))

    def w_rows(half, owner, at):
        return wbuf.at[half, owner, pl.ds(at * part, part)]

    def w_start(half, at, step):
        src = weight.at[0, pl.ds(at * part, part), pl.ds(half * head, head)]
        target = sib if step == 0 else peer(step)
        send(src, w_rows(half, me, at), w_send.at[half, step, at], w_recv.at[half, step, at],
             {"seq": target})

    def w_arrived(half, at, step):
        owner = sib if step == 0 else peer(chips - step)
        arrived(w_rows(half, owner, at), w_send.at[half, step, at], w_recv.at[half, step, at])
        return owner

    def project(half, owner, at):
        cols = pl.ds(pl.multiple_of(owner * rows + at * part, 128), part)
        acc[...] += dot(tok[:, cols], wbuf[half, owner, pl.ds(at * part, part)], ((1,), (0,)))

    def gather_chunk(half, at):
        for step in range(1, chips):
            owner = w_arrived(half, at, step)
            send(w_rows(half, owner, at), w_rows(half, owner, at), fwd_send.at[half, step, at],
                 fwd_recv.at[half, step, at], {"seq": sib})
            project(half, owner, at)
            if half == 0:
                w_start(1, at, step)
        for step in range(1, chips):
            owner = peer_sib(chips - step)
            arrived(w_rows(half, owner, at), fwd_send.at[half, step, at], fwd_recv.at[half, step, at])
            project(half, owner, at)

    for at in range(CHUNKS):
        for step in range(1, chips):
            w_start(0, at, step)
    for half in range(2):
        for at in range(CHUNKS):
            w_start(half, at, 0)

    def kv_share(half):
        kvbuf[half, me] = acc[...].astype(BF16)
        for step in range(1, seq_count):
            send(kvbuf.at[half, me], kvbuf.at[half, me], kv_send.at[half, step],
                 kv_recv.at[half, step], {"seq": seq_other(step)})

    def kv_collect(half):
        for step in range(1, seq_count):
            owner = seq_other(seq_count - step)
            arrived(kvbuf.at[half, owner], kv_send.at[half, step], kv_recv.at[half, step])

    def terms_share(half):
        for step in range(1, seq_count):
            owner = seq_other(step)
            send(terms_out.at[half, owner], terms_in.at[half, step], term_send.at[half, step],
                 term_recv.at[half, step], {"seq": owner})

    def terms_collect(half):
        total = terms_out[half, me].astype(F32)
        for step in range(1, seq_count):
            arrived(terms_in.at[half, step], term_send.at[half, step], term_recv.at[half, step])
            total += terms_in[half, step].astype(F32)
        kv_grad[half] = total.astype(BF16)

    def start_half(half):
        own_copies[half].wait()
        acc[...] = jnp.zeros_like(acc)
        for at in range(CHUNKS):
            project(half, me, at)
        for at in range(CHUNKS):
            project(half, w_arrived(half, at, 0), at)

    tok_copy.wait()
    start_half(0)
    for at in range(CHUNKS):
        gather_chunk(0, at)
    kv_share(0)
    start_half(1)
    gather_chunk(1, 0)

    kv_collect(0)
    key_len = seq_count * n_tok
    blocks_here = n_tok // BLOCK
    scale = F32(inv_root)
    for blk in range(blocks_here):
        span = pl.ds(blk * BLOCK, BLOCK)
        block = me * blocks_here + blk
        key_block = lax.div(lax.broadcasted_iota(jnp.int32, (BLOCK, key_len), 1), jnp.int32(BLOCK))
        allowed = (jnp.abs(key_block - block) <= 1) | (key_block == 0)
        for choice in range(rand.shape[1]):
            allowed = allowed | (key_block == rand[block, choice])
        scores = dot(query[0, span, :], kvbuf[0].reshape(key_len, head), ((1,), (1,))) * scale
        unnorm = jnp.where(allowed, jnp.exp(scores), F32(0.0))
        prob[span, :] = unnorm / jnp.sum(unnorm, axis=1, keepdims=True)
    for owner in range(seq_count):
        cols = pl.ds(owner * n_tok, n_tok)
        terms_out[1, owner] = dot(prob[:, cols].astype(BF16), grad[0], ((0,), (0,))).astype(BF16)
    terms_share(1)

    for at in range(1, CHUNKS):
        gather_chunk(1, at)
    kv_share(1)

    def product(half, owner, at):
        cols = pl.ds(pl.multiple_of(owner * rows + at * part, 128), part)
        return dot(tok[:, cols], kv_grad[half], ((0,), (0,)))

    def chunk(at):
        return pl.ds(at * part, part)

    def to_sib(half, at, step):
        sib_out[half, step, chunk(at)] = product(half, peer_sib(step), at).astype(BF16)
        send(sib_out.at[half, step, chunk(at)], sib_in.at[half, step, chunk(at)],
             sib_send.at[half, step, at], sib_recv.at[half, step, at], {"seq": sib})

    def with_sib(half, at, step):
        own = product(half, peer(step), at)
        arrived(sib_in.at[half, step, chunk(at)], sib_send.at[half, step, at],
                sib_recv.at[half, step, at])
        return own + sib_in[half, step, chunk(at)].astype(F32)

    def to_peer(half, at, step):
        peer_out[half, step, chunk(at)] = with_sib(half, at, step).astype(BF16)
        send(peer_out.at[half, step, chunk(at)], peer_in.at[half, step, chunk(at)],
             peer_send.at[half, step, at], peer_recv.at[half, step, at], {"seq": peer(step)})

    def reduce_first(half):
        for at in range(CHUNKS):
            for step in range(1, chips):
                to_sib(half, at, step)
        for step in range(1, chips):
            to_peer(half, 0, step)

    def reduce_rest(half):
        for at in range(1, CHUNKS):
            for step in range(1, chips):
                to_peer(half, at, step)
        for at in range(CHUNKS):
            to_sib(half, at, 0)

    def gossip_send(src, half, at, slot, partner):
        send(src.at[half, chunk(at)], gossip_in.at[slot, half, chunk(at)],
             gos_send.at[slot, half, at], gos_recv.at[slot, half, at], {"rep": partner})

    def gossip_arrived(half, at, slot):
        arrived(gossip_in.at[slot, half, chunk(at)], gos_send.at[slot, half, at],
                gos_recv.at[slot, half, at])
        return gossip_in[slot, half, chunk(at)].astype(F32)

    def out_at(half, at):
        return (0, chunk(at), pl.ds(half * head, head))

    def reduce_end(half, at):
        total = with_sib(half, at, 0)
        for step in range(1, chips):
            arrived(peer_in.at[half, step, chunk(at)], peer_send.at[half, step, at],
                    peer_recv.at[half, step, at])
            total += peer_in[half, step, chunk(at)].astype(F32)
        mixed[out_at(half, at)] = total
        if dist:
            gossip_out[half, chunk(at)] = total.astype(BF16)
            for slot in range(1 if two_step else len(partners)):
                gossip_send(gossip_out, half, at, slot, partners[slot])

    def gossip_relay(half, at):
        if two_step:
            total = mixed[out_at(half, at)] + gossip_arrived(half, at, 0)
            relay_out[half, chunk(at)] = total.astype(BF16)
            gossip_send(relay_out, half, at, 1, pair_rep)

    def gossip_end(half, at):
        own = mixed[out_at(half, at)]
        if dist == 0:
            total = own + own + own
        elif two_step:
            total = own + gossip_arrived(half, at, 1)
        elif len(partners) == 1:
            other = gossip_arrived(half, at, 0)
            total = own + other + other
        else:
            total = own + gossip_arrived(half, at, 0) + gossip_arrived(half, at, 1)
        mixed[out_at(half, at)] = total / F32(3.0)

    terms_collect(1)
    reduce_first(1)

    kv_collect(1)
    values = kvbuf[1].reshape(key_len, head)
    keys = kvbuf[0].reshape(key_len, head)
    for blk in range(blocks_here):
        span = pl.ds(blk * BLOCK, BLOCK)
        prob_rows = prob[span, :]
        grad_rows = grad[0, span, :]
        context = dot(prob_rows.astype(BF16), values, ((1,), (0,)))
        delta = jnp.sum(grad_rows.astype(F32) * context, axis=1, keepdims=True)
        prob_grad = dot(grad_rows, values, ((1,), (1,)))
        score_grad = prob_rows * (prob_grad - delta) * scale
        prob[span, :] = score_grad
        query_grad[0, span, :] = dot(score_grad.astype(BF16), keys, ((1,), (0,))).astype(BF16)
    for owner in range(seq_count):
        cols = pl.ds(owner * n_tok, n_tok)
        terms_out[0, owner] = dot(prob[:, cols].astype(BF16), query[0], ((0,), (0,))).astype(BF16)
    terms_share(0)

    reduce_rest(1)
    terms_collect(0)
    reduce_first(0)
    reduce_end(1, 0)
    reduce_rest(0)
    for at in range(1, CHUNKS):
        reduce_end(1, at)
    for at in range(CHUNKS):
        gossip_relay(1, at)
    for at in range(CHUNKS):
        reduce_end(0, at)
    for at in range(CHUNKS):
        gossip_relay(0, at)
    for half in (1, 0):
        for at in range(CHUNKS):
            gossip_end(half, at)
    for copy in sent:
        copy.wait_send()


def fused(tokens, queries, ctx_grad, kv_weight, rand_blocks, dist, ident):
    seq_count = lax.axis_size("seq")
    rep_count = lax.axis_size("rep")
    _, n_tok, width = tokens.shape
    _, rows, kv_width = kv_weight.shape
    head = kv_width // 2
    chips = seq_count // 2
    dma = pltpu.SemaphoreType.DMA
    vmem = pl.BlockSpec(memory_space=pltpu.VMEM)
    anywhere = pl.BlockSpec(memory_space=pl.ANY)
    per_chip = dma((2, chips, CHUNKS))
    per_seq = dma((2, seq_count))
    return pl.pallas_call(
        partial(kernel, dist, rep_count, seq_count),
        out_shape=(
            jax.ShapeDtypeStruct((1, rows, kv_width), F32),
            jax.ShapeDtypeStruct(queries.shape, BF16),
        ),
        in_specs=[anywhere, vmem, vmem, anywhere, pl.BlockSpec(memory_space=pltpu.SMEM)],
        out_specs=(vmem, vmem),
        scratch_shapes=[
            pltpu.VMEM((n_tok, width), BF16),
            pltpu.VMEM((2, seq_count, rows, head), BF16),
            pltpu.VMEM((2, seq_count, n_tok, head), BF16),
            pltpu.VMEM((n_tok, seq_count * n_tok), F32),
            pltpu.VMEM((2, seq_count, n_tok, head), BF16),
            pltpu.VMEM((2, seq_count, n_tok, head), BF16),
            pltpu.VMEM((2, n_tok, head), BF16),
            pltpu.VMEM((n_tok, head), F32),
            pltpu.VMEM((2, chips, rows, head), BF16),
            pltpu.VMEM((2, chips, rows, head), BF16),
            pltpu.VMEM((2, chips, rows, head), BF16),
            pltpu.VMEM((2, chips, rows, head), BF16),
            pltpu.VMEM((2, rows, head), BF16),
            pltpu.VMEM((2, 2, rows, head), BF16),
            pltpu.VMEM((2, rows, head), BF16),
            dma((3,)),
            per_chip, per_chip, per_chip, per_chip,
            per_seq, per_seq, per_seq, per_seq,
            per_chip, per_chip, per_chip, per_chip,
            dma((2, 2, CHUNKS)), dma((2, 2, CHUNKS)),
        ],
        compiler_params=pltpu.CompilerParams(
            collective_id=ident, has_side_effects=True, vmem_limit_bytes=48 * 1024 * 1024
        ),
    )(tokens, queries, ctx_grad, kv_weight, rand_blocks)


def per_device(tokens, queries, ctx_grad, kv_weight, rand_blocks, step_count):
    rep_count = lax.axis_size("rep")
    branches = [
        partial(fused, dist=(1 << level) % rep_count, ident=level) for level in range(4)
    ]
    return lax.switch(
        step_count[0] % 4, branches, tokens, queries, ctx_grad, kv_weight, rand_blocks
    )


def solution(mesh):
    return jax.shard_map(
        per_device,
        mesh=mesh,
        in_specs=(
            P("rep", "seq", None),
            P("rep", "seq", None),
            P("rep", "seq", None),
            P("rep", "seq", None),
            P(),
            P(),
        ),
        out_specs=(P("rep", "seq", None), P("rep", "seq", None)),
        check_vma=False,
    )
```

```python
from functools import partial

import jax
import jax.numpy as jnp
from jax import lax
from jax.experimental import pallas as pl
from jax.experimental.pallas import tpu as pltpu
from jax.sharding import PartitionSpec as P

BLOCK = 64
TILE = 384
MESH = pl.DeviceIdType.MESH
BF16 = jnp.bfloat16
F32 = jnp.float32


def chunks_of(rows):
    return 2 if rows % (2 * TILE) == 0 else 1


def dot(a, b, dims):
    return lax.dot_general(a, b, (dims, ((), ())), preferred_element_type=F32)


def kernel(
    dist, rep_count, seq_count,
    tok_hbm, query, grad, weight, rand,
    mixed, query_grad,
    tok, turned, wbuf, kvbuf, prob, terms_out, terms_in, kv_grad, acc,
    sib_out, sib_in, peer_out, peer_in, gossip_out, gossip_in, relay_out,
    local_sem, w_send, w_recv, fwd_send, fwd_recv, kv_send, kv_recv, term_send, term_recv,
    sib_send, sib_recv, peer_send, peer_recv, gos_send, gos_recv,
):
    n_tok = tok.shape[0]
    rows = wbuf.shape[2]
    head = wbuf.shape[3]
    count = chunks_of(rows)
    part = rows // count
    tiles = part // TILE
    chips = seq_count // 2
    inv_root = head ** (-0.5)
    rep = lax.axis_index("rep")
    me = lax.axis_index("seq")
    chip, core = me // 2, me % 2
    sib = chip * 2 + (1 - core)

    def loop(total, body):
        if total == 1:
            body(0)
        else:
            lax.fori_loop(0, total, lambda at, carry: (body(at), carry)[1], 0)

    def tile_loop(start, total, body):
        loop(total, lambda tile: body(pl.ds(pl.multiple_of(start + tile * TILE, 128), TILE)))

    def seq_other(step):
        return lax.rem(me + step, seq_count)

    def peer(step):
        return lax.rem(chip + step, chips) * 2 + core

    def peer_sib(step):
        return lax.rem(chip + step, chips) * 2 + (1 - core)

    def send(src, dst, send_sem, recv_sem, target):
        copy = pltpu.make_async_remote_copy(
            src_ref=src, dst_ref=dst, send_sem=send_sem, recv_sem=recv_sem,
            device_id=target, device_id_type=MESH,
        )
        copy.start()

    def left(ref, send_sem, recv_sem):
        pltpu.make_async_remote_copy(
            src_ref=ref, dst_ref=ref, send_sem=send_sem, recv_sem=recv_sem,
            device_id={"seq": sib}, device_id_type=MESH,
        ).wait_send()

    def arrived(ref, send_sem, recv_sem):
        pltpu.make_async_remote_copy(
            src_ref=ref, dst_ref=ref, send_sem=send_sem, recv_sem=recv_sem,
            device_id={"seq": sib}, device_id_type=MESH,
        ).wait_recv()

    two_step = dist == 1 and rep_count % 2 == 0 and rep_count > 2
    if dist == 0:
        partners = []
    elif two_step:
        side = rep % 2
        next_rep = lax.rem(rep + rep_count + 4 * side - 2, rep_count)
        prev_rep = lax.rem(rep + rep_count - 4 * side + 2, rep_count)
        pair_rep = rep + 1 - 2 * side
        partners = [next_rep, prev_rep, pair_rep] if rep_count > 4 else [next_rep, pair_rep]
    elif 2 * dist % rep_count == 0:
        partners = [lax.rem(rep + dist, rep_count)]
    else:
        partners = [lax.rem(rep + dist, rep_count), lax.rem(rep + rep_count - dist, rep_count)]

    tok_copy = pltpu.make_async_copy(tok_hbm.at[0], tok, local_sem.at[0])
    tok_copy.start()
    own_copies = []
    for half in range(2):
        copy = pltpu.make_async_copy(
            weight.at[0, :, pl.ds(half * head, head)], wbuf.at[half, me], local_sem.at[1 + half]
        )
        copy.start()
        own_copies.append(copy)

    barrier = pltpu.get_barrier_semaphore()
    for step in range(1, seq_count):
        pl.semaphore_signal(barrier, inc=1, device_id={"seq": seq_other(step)}, device_id_type=MESH)
    for partner in partners:
        pl.semaphore_signal(barrier, inc=1, device_id={"rep": partner}, device_id_type=MESH)
    pl.semaphore_wait(barrier, seq_count - 1 + len(partners))

    def w_rows(half, owner, at):
        return wbuf.at[half, owner, pl.ds(at * part, part)]

    def w_start(half, at, step):
        src = weight.at[0, pl.ds(at * part, part), pl.ds(half * head, head)]
        target = sib if step == 0 else peer(step)
        send(src, w_rows(half, me, at), w_send.at[half, step, at], w_recv.at[half, step, at],
             {"seq": target})

    def w_arrived(half, at, step):
        owner = sib if step == 0 else peer(chips - step)
        arrived(w_rows(half, owner, at), w_send.at[half, step, at], w_recv.at[half, step, at])
        return owner

    def project(half, owner, at):
        def body(span):
            cols = pl.ds(pl.multiple_of(owner * rows + span.start, 128), TILE)
            acc[...] += dot(tok[:, cols], wbuf[half, owner, span], ((1,), (0,)))

        tile_loop(at * part, tiles, body)

    def gather_chunk(half, at):
        for step in range(1, chips):
            owner = w_arrived(half, at, step)
            send(w_rows(half, owner, at), w_rows(half, owner, at), fwd_send.at[half, step, at],
                 fwd_recv.at[half, step, at], {"seq": sib})
            project(half, owner, at)
            if half == 0:
                w_start(1, at, step)
        for step in range(1, chips):
            owner = peer_sib(chips - step)
            arrived(w_rows(half, owner, at), fwd_send.at[half, step, at], fwd_recv.at[half, step, at])
            project(half, owner, at)

    for at in range(count):
        for step in range(1, chips):
            w_start(0, at, step)
    for half in range(2):
        for at in range(count):
            w_start(half, at, 0)

    def kv_share(half):
        kvbuf[half, me] = acc[...].astype(BF16)
        for step in range(1, seq_count):
            send(kvbuf.at[half, me], kvbuf.at[half, me], kv_send.at[half, step],
                 kv_recv.at[half, step], {"seq": seq_other(step)})

    def kv_collect(half):
        for step in range(1, seq_count):
            owner = seq_other(seq_count - step)
            arrived(kvbuf.at[half, owner], kv_send.at[half, step], kv_recv.at[half, step])

    def terms_share(half):
        for step in range(1, seq_count):
            owner = seq_other(step)
            send(terms_out.at[half, owner], terms_in.at[half, step], term_send.at[half, step],
                 term_recv.at[half, step], {"seq": owner})

    def terms_collect(half):
        total = terms_out[half, me].astype(F32)
        for step in range(1, seq_count):
            arrived(terms_in.at[half, step], term_send.at[half, step], term_recv.at[half, step])
            total += terms_in[half, step].astype(F32)
        kv_grad[half] = total.astype(BF16)

    def start_half(half):
        own_copies[half].wait()
        for at in range(count):
            w_arrived(half, at, 0)
        acc[...] = jnp.zeros_like(acc)

        def body(at):
            project(half, chip * 2 + at // count, at % count)

        loop(2 * count, body)

    tok_copy.wait()

    def turn(span):
        turned[span, :] = tok[:, span].T

    tile_loop(0, tok.shape[1] // TILE, turn)
    start_half(0)
    loop(count, lambda at: gather_chunk(0, at))
    kv_share(0)
    start_half(1)
    gather_chunk(1, 0)

    kv_collect(0)
    key_len = seq_count * n_tok
    blocks_here = n_tok // BLOCK
    scale = F32(inv_root)
    def probabilities(blk):
        span = pl.ds(pl.multiple_of(blk * BLOCK, BLOCK), BLOCK)
        block = me * blocks_here + blk
        key_block = lax.div(lax.broadcasted_iota(jnp.int32, (BLOCK, key_len), 1), jnp.int32(BLOCK))
        allowed = (jnp.abs(key_block - block) <= 1) | (key_block == 0)
        for choice in range(rand.shape[1]):
            allowed = allowed | (key_block == rand[block, choice])
        scores = dot(query[0, span, :], kvbuf[0].reshape(key_len, head), ((1,), (1,))) * scale
        unnorm = jnp.where(allowed, jnp.exp(scores), F32(0.0))
        prob[span, :] = unnorm / jnp.sum(unnorm, axis=1, keepdims=True)
    loop(blocks_here, probabilities)

    def terms(half, other):
        def body(owner):
            cols = pl.ds(pl.multiple_of(owner * n_tok, n_tok), n_tok)
            terms_out[half, owner] = dot(
                prob[:, cols].astype(BF16), other[0], ((0,), (0,))
            ).astype(BF16)

        loop(seq_count, body)

    terms(1, grad)
    terms_share(1)

    for at in range(1, count):
        gather_chunk(1, at)
    kv_share(1)

    def product(half, owner, span):
        src = pl.ds(pl.multiple_of(owner * rows + span.start, 128), TILE)
        return dot(turned[src, :], kv_grad[half], ((1,), (0,)))

    def chunk(at):
        return pl.ds(pl.multiple_of(at * part, 128), part)

    def to_sib(half, at, step):
        owner = peer_sib(step)

        def body(span):
            sib_out[half, step, span] = product(half, owner, span).astype(BF16)

        tile_loop(at * part, tiles, body)
        send(sib_out.at[half, step, chunk(at)], sib_in.at[half, step, chunk(at)],
             sib_send.at[half, step, at], sib_recv.at[half, step, at], {"seq": sib})

    def sib_arrived(half, at, step):
        arrived(sib_in.at[half, step, chunk(at)], sib_send.at[half, step, at],
                sib_recv.at[half, step, at])

    def to_peer(half, at, step):
        owner = peer(step)
        sib_arrived(half, at, step)

        def body(span):
            total = product(half, owner, span) + sib_in[half, step, span].astype(F32)
            peer_out[half, step, span] = total.astype(BF16)

        tile_loop(at * part, tiles, body)
        send(peer_out.at[half, step, chunk(at)], peer_in.at[half, step, chunk(at)],
             peer_send.at[half, step, at], peer_recv.at[half, step, at], {"seq": owner})

    def reduce_first(half):
        for step in range(1, chips):
            loop(count, lambda at: to_sib(half, at, step))
        for step in range(1, chips):
            to_peer(half, 0, step)

    def reduce_rest(half):
        for at in range(1, count):
            for step in range(1, chips):
                to_peer(half, at, step)
        loop(count, lambda at: to_sib(half, at, 0))

    def gossip_send(src, half, at, slot, partner):
        send(src.at[half, chunk(at)], gossip_in.at[slot, half, chunk(at)],
             gos_send.at[slot, half, at], gos_recv.at[slot, half, at], {"rep": partner})

    def gossip_arrived(half, at, slot):
        arrived(gossip_in.at[slot, half, chunk(at)], gos_send.at[slot, half, at],
                gos_recv.at[slot, half, at])

    def cols_of(half):
        return pl.ds(pl.multiple_of(half * head, 128), head)

    def reduce_end(half, at):
        sib_arrived(half, at, 0)
        for step in range(1, chips):
            arrived(peer_in.at[half, step, chunk(at)], peer_send.at[half, step, at],
                    peer_recv.at[half, step, at])

        def body(span):
            total = product(half, me, span) + sib_in[half, 0, span].astype(F32)
            for step in range(1, chips):
                total += peer_in[half, step, span].astype(F32)
            mixed[0, span, cols_of(half)] = total
            if dist:
                gossip_out[half, span] = total.astype(BF16)

        tile_loop(at * part, tiles, body)
        if dist:
            for slot in range(1 if two_step else len(partners)):
                gossip_send(gossip_out, half, at, slot, partners[slot])

    def gossip_relay(half, at):
        if two_step:
            gossip_arrived(half, at, 0)

            def body(span):
                total = mixed[0, span, cols_of(half)] + gossip_in[0, half, span].astype(F32)
                relay_out[half, span] = total.astype(BF16)

            tile_loop(at * part, tiles, body)
            gossip_send(relay_out, half, at, 1, pair_rep)

    def gossip_end(half, at):
        slots = [] if dist == 0 else [1] if two_step else list(range(len(partners)))
        for slot in slots:
            gossip_arrived(half, at, slot)

        def body(span):
            own = mixed[0, span, cols_of(half)]
            if dist == 0:
                total = own + own + own
            elif two_step:
                total = own + gossip_in[1, half, span].astype(F32)
            elif len(partners) == 1:
                other = gossip_in[0, half, span].astype(F32)
                total = own + other + other
            else:
                total = own + gossip_in[0, half, span].astype(F32)
                total += gossip_in[1, half, span].astype(F32)
            mixed[0, span, cols_of(half)] = total / F32(3.0)

        tile_loop(at * part, tiles, body)

    terms_collect(1)
    reduce_first(1)

    kv_collect(1)
    def score_grads(blk):
        span = pl.ds(pl.multiple_of(blk * BLOCK, BLOCK), BLOCK)
        values = kvbuf[1].reshape(key_len, head)
        keys = kvbuf[0].reshape(key_len, head)
        prob_rows = prob[span, :]
        grad_rows = grad[0, span, :]
        context = dot(prob_rows.astype(BF16), values, ((1,), (0,)))
        delta = jnp.sum(grad_rows.astype(F32) * context, axis=1, keepdims=True)
        prob_grad = dot(grad_rows, values, ((1,), (1,)))
        score_grad = prob_rows * (prob_grad - delta) * scale
        prob[span, :] = score_grad
        query_grad[0, span, :] = dot(score_grad.astype(BF16), keys, ((1,), (0,))).astype(BF16)
    loop(blocks_here, score_grads)
    terms(0, query)
    terms_share(0)

    reduce_rest(1)
    terms_collect(0)
    reduce_first(0)
    reduce_end(1, 0)
    reduce_rest(0)
    for at in range(1, count):
        reduce_end(1, at)
    loop(count, lambda at: gossip_relay(1, at))
    loop(count, lambda at: reduce_end(0, at))
    loop(count, lambda at: gossip_relay(0, at))
    loop(2 * count, lambda item: gossip_end(1 - item // count, item % count))

    def drain(half):
        def drain_chunk(at):
            rows_at = w_rows(half, me, at)
            for step in range(chips):
                left(rows_at, w_send.at[half, step, at], w_recv.at[half, step, at])
                left(rows_at, sib_send.at[half, step, at], sib_recv.at[half, step, at])
            for step in range(1, chips):
                left(rows_at, fwd_send.at[half, step, at], fwd_recv.at[half, step, at])
                left(rows_at, peer_send.at[half, step, at], peer_recv.at[half, step, at])
            for slot in range(0 if dist == 0 else 2 if two_step else len(partners)):
                left(rows_at, gos_send.at[slot, half, at], gos_recv.at[slot, half, at])

        loop(count, drain_chunk)
        for step in range(1, seq_count):
            left(kvbuf.at[half, me], kv_send.at[half, step], kv_recv.at[half, step])
            left(kvbuf.at[half, me], term_send.at[half, step], term_recv.at[half, step])

    loop(2, drain)


def fused(tokens, queries, ctx_grad, kv_weight, rand_blocks, dist, ident):
    seq_count = lax.axis_size("seq")
    rep_count = lax.axis_size("rep")
    _, n_tok, width = tokens.shape
    _, rows, kv_width = kv_weight.shape
    head = kv_width // 2
    chips = seq_count // 2
    count = chunks_of(rows)
    dma = pltpu.SemaphoreType.DMA
    vmem = pl.BlockSpec(memory_space=pltpu.VMEM)
    anywhere = pl.BlockSpec(memory_space=pl.ANY)
    per_chip = dma((2, chips, count))
    per_seq = dma((2, seq_count))
    return pl.pallas_call(
        partial(kernel, dist, rep_count, seq_count),
        out_shape=(
            jax.ShapeDtypeStruct((1, rows, kv_width), F32),
            jax.ShapeDtypeStruct(queries.shape, BF16),
        ),
        in_specs=[anywhere, vmem, vmem, anywhere, pl.BlockSpec(memory_space=pltpu.SMEM)],
        out_specs=(vmem, vmem),
        scratch_shapes=[
            pltpu.VMEM((n_tok, width), BF16),
            pltpu.VMEM((width, n_tok), BF16),
            pltpu.VMEM((2, seq_count, rows, head), BF16),
            pltpu.VMEM((2, seq_count, n_tok, head), BF16),
            pltpu.VMEM((n_tok, seq_count * n_tok), F32),
            pltpu.VMEM((2, seq_count, n_tok, head), BF16),
            pltpu.VMEM((2, seq_count, n_tok, head), BF16),
            pltpu.VMEM((2, n_tok, head), BF16),
            pltpu.VMEM((n_tok, head), F32),
            pltpu.VMEM((2, chips, rows, head), BF16),
            pltpu.VMEM((2, chips, rows, head), BF16),
            pltpu.VMEM((2, chips, rows, head), BF16),
            pltpu.VMEM((2, chips, rows, head), BF16),
            pltpu.VMEM((2, rows, head), BF16),
            pltpu.VMEM((2, 2, rows, head), BF16),
            pltpu.VMEM((2, rows, head), BF16),
            dma((3,)),
            per_chip, per_chip, per_chip, per_chip,
            per_seq, per_seq, per_seq, per_seq,
            per_chip, per_chip, per_chip, per_chip,
            dma((2, 2, count)), dma((2, 2, count)),
        ],
        compiler_params=pltpu.CompilerParams(
            collective_id=ident, has_side_effects=True, vmem_limit_bytes=48 * 1024 * 1024
        ),
    )(tokens, queries, ctx_grad, kv_weight, rand_blocks)


def per_device(tokens, queries, ctx_grad, kv_weight, rand_blocks, step_count):
    rep_count = lax.axis_size("rep")
    branches = [
        partial(fused, dist=(1 << level) % rep_count, ident=level) for level in range(4)
    ]
    return lax.switch(
        step_count[0] % 4, branches, tokens, queries, ctx_grad, kv_weight, rand_blocks
    )


def solution(mesh):
    return jax.shard_map(
        per_device,
        mesh=mesh,
        in_specs=(
            P("rep", "seq", None),
            P("rep", "seq", None),
            P("rep", "seq", None),
            P("rep", "seq", None),
            P(),
            P(),
        ),
        out_specs=(P("rep", "seq", None), P("rep", "seq", None)),
        check_vma=False,
    )
```

```python
from functools import partial

import jax
import jax.numpy as jnp
from jax import lax
from jax.experimental import pallas as pl
from jax.experimental.pallas import tpu as pltpu
from jax.sharding import PartitionSpec as P

BLOCK = 64
TILE = 384
MESH = pl.DeviceIdType.MESH
BF16 = jnp.bfloat16
F32 = jnp.float32


def chunks_of(rows):
    return 2 if rows % (2 * TILE) == 0 else 1


def dot(a, b, dims):
    return lax.dot_general(a, b, (dims, ((), ())), preferred_element_type=F32)


def kernel(
    dist, rep_count, seq_count,
    tok_hbm, query, grad, weight, rand,
    mixed, query_grad,
    tok, turned, wbuf, kvbuf, prob, terms_out, terms_in, sums_out, sums_in, kv_grad, acc,
    sib_out, sib_in, peer_out, peer_in, gossip_out, gossip_in, relay_out,
    local_sem, w_send, w_recv, fwd_send, fwd_recv, kv_send, kv_recv,
    kv_fwd_send, kv_fwd_recv, term_send, term_recv, sum_send, sum_recv,
    sib_send, sib_recv, peer_send, peer_recv, gos_send, gos_recv,
):
    n_tok = tok.shape[0]
    rows = wbuf.shape[2]
    head = wbuf.shape[3]
    count = chunks_of(rows)
    part = rows // count
    tiles = part // TILE
    chips = seq_count // 2
    inv_root = head ** (-0.5)
    rep = lax.axis_index("rep")
    me = lax.axis_index("seq")
    chip, core = me // 2, me % 2
    sib = chip * 2 + (1 - core)

    def loop(total, body):
        if total == 1:
            body(0)
        else:
            lax.fori_loop(0, total, lambda at, carry: (body(at), carry)[1], 0)

    def tile_loop(start, total, body):
        loop(total, lambda tile: body(pl.ds(pl.multiple_of(start + tile * TILE, 128), TILE)))

    def peer(step):
        return lax.rem(chip + step, chips) * 2 + core

    def peer_sib(step):
        return lax.rem(chip + step, chips) * 2 + (1 - core)

    def send(src, dst, send_sem, recv_sem, target):
        copy = pltpu.make_async_remote_copy(
            src_ref=src, dst_ref=dst, send_sem=send_sem, recv_sem=recv_sem,
            device_id=target, device_id_type=MESH,
        )
        copy.start()

    def left(ref, send_sem, recv_sem):
        pltpu.make_async_remote_copy(
            src_ref=ref, dst_ref=ref, send_sem=send_sem, recv_sem=recv_sem,
            device_id={"seq": sib}, device_id_type=MESH,
        ).wait_send()

    def arrived(ref, send_sem, recv_sem):
        pltpu.make_async_remote_copy(
            src_ref=ref, dst_ref=ref, send_sem=send_sem, recv_sem=recv_sem,
            device_id={"seq": sib}, device_id_type=MESH,
        ).wait_recv()

    two_step = dist == 1 and rep_count % 2 == 0 and rep_count > 2
    if dist == 0:
        partners = []
    elif two_step:
        side = rep % 2
        next_rep = lax.rem(rep + rep_count + 4 * side - 2, rep_count)
        prev_rep = lax.rem(rep + rep_count - 4 * side + 2, rep_count)
        pair_rep = rep + 1 - 2 * side
        partners = [next_rep, prev_rep, pair_rep] if rep_count > 4 else [next_rep, pair_rep]
    elif 2 * dist % rep_count == 0:
        partners = [lax.rem(rep + dist, rep_count)]
    else:
        partners = [lax.rem(rep + dist, rep_count), lax.rem(rep + rep_count - dist, rep_count)]

    tok_copy = pltpu.make_async_copy(tok_hbm.at[0], tok, local_sem.at[0])
    tok_copy.start()
    own_copies = []
    for half in range(2):
        copy = pltpu.make_async_copy(
            weight.at[0, :, pl.ds(half * head, head)], wbuf.at[half, me], local_sem.at[1 + half]
        )
        copy.start()
        own_copies.append(copy)

    barrier = pltpu.get_barrier_semaphore()
    for step in range(chips):
        target = peer(step) if step else sib
        pl.semaphore_signal(barrier, inc=1, device_id={"seq": target}, device_id_type=MESH)
    for partner in partners:
        pl.semaphore_signal(barrier, inc=1, device_id={"rep": partner}, device_id_type=MESH)
    pl.semaphore_wait(barrier, chips + len(partners))

    def w_rows(half, owner, at):
        return wbuf.at[half, owner, pl.ds(at * part, part)]

    def w_start(half, at, step):
        src = weight.at[0, pl.ds(at * part, part), pl.ds(half * head, head)]
        target = sib if step == 0 else peer(step)
        send(src, w_rows(half, me, at), w_send.at[half, step, at], w_recv.at[half, step, at],
             {"seq": target})

    def w_arrived(half, at, step):
        owner = sib if step == 0 else peer(chips - step)
        arrived(w_rows(half, owner, at), w_send.at[half, step, at], w_recv.at[half, step, at])
        return owner

    def project(half, owner, at):
        def body(span):
            cols = pl.ds(pl.multiple_of(owner * rows + span.start, 128), TILE)
            acc[...] += dot(tok[:, cols], wbuf[half, owner, span], ((1,), (0,)))

        tile_loop(at * part, tiles, body)

    def gather_chunk(half, at):
        for step in range(1, chips):
            owner = w_arrived(half, at, step)
            send(w_rows(half, owner, at), w_rows(half, owner, at), fwd_send.at[half, step, at],
                 fwd_recv.at[half, step, at], {"seq": sib})
            project(half, owner, at)
            if half == 0:
                w_start(1, at, step)
        for step in range(1, chips):
            owner = peer_sib(chips - step)
            arrived(w_rows(half, owner, at), fwd_send.at[half, step, at], fwd_recv.at[half, step, at])
            project(half, owner, at)

    for at in range(count):
        for step in range(1, chips):
            w_start(0, at, step)
    for half in range(2):
        for at in range(count):
            w_start(half, at, 0)

    def kv_share(half):
        kvbuf[half, me] = acc[...].astype(BF16)
        for step in range(chips):
            send(kvbuf.at[half, me], kvbuf.at[half, me], kv_send.at[half, step],
                 kv_recv.at[half, step], {"seq": peer(step) if step else sib})

    def kv_collect(half):
        for step in range(1, chips):
            owner = peer(chips - step)
            arrived(kvbuf.at[half, owner], kv_send.at[half, step], kv_recv.at[half, step])
            send(kvbuf.at[half, owner], kvbuf.at[half, owner], kv_fwd_send.at[half, step],
                 kv_fwd_recv.at[half, step], {"seq": sib})
        arrived(kvbuf.at[half, sib], kv_send.at[half, 0], kv_recv.at[half, 0])
        for step in range(1, chips):
            owner = peer_sib(chips - step)
            arrived(kvbuf.at[half, owner], kv_fwd_send.at[half, step], kv_fwd_recv.at[half, step])

    def terms_share(half):
        for step in list(range(1, chips)) + [0]:
            send(terms_out.at[half, peer_sib(step)], terms_in.at[half, step],
                 term_send.at[half, step], term_recv.at[half, step], {"seq": sib})
        for step in range(1, chips):
            arrived(terms_in.at[half, step], term_send.at[half, step], term_recv.at[half, step])
            total = terms_out[half, peer(step)].astype(F32) + terms_in[half, step].astype(F32)
            sums_out[half, step] = total.astype(BF16)
            send(sums_out.at[half, step], sums_in.at[half, step], sum_send.at[half, step],
                 sum_recv.at[half, step], {"seq": peer(step)})

    def terms_collect(half):
        arrived(terms_in.at[half, 0], term_send.at[half, 0], term_recv.at[half, 0])
        total = terms_out[half, me].astype(F32) + terms_in[half, 0].astype(F32)
        for step in range(1, chips):
            arrived(sums_in.at[half, step], sum_send.at[half, step], sum_recv.at[half, step])
            total += sums_in[half, step].astype(F32)
        kv_grad[half] = total.astype(BF16)

    def start_half(half):
        own_copies[half].wait()
        for at in range(count):
            w_arrived(half, at, 0)
        acc[...] = jnp.zeros_like(acc)

        def body(at):
            project(half, chip * 2 + at // count, at % count)

        loop(2 * count, body)

    tok_copy.wait()

    def turn(span):
        turned[span, :] = tok[:, span].T

    tile_loop(0, tok.shape[1] // TILE, turn)
    start_half(0)
    loop(count, lambda at: gather_chunk(0, at))
    kv_share(0)
    start_half(1)
    gather_chunk(1, 0)

    kv_collect(0)
    key_len = seq_count * n_tok
    blocks_here = n_tok // BLOCK
    scale = F32(inv_root)
    def probabilities(blk):
        span = pl.ds(pl.multiple_of(blk * BLOCK, BLOCK), BLOCK)
        block = me * blocks_here + blk
        key_block = lax.div(lax.broadcasted_iota(jnp.int32, (BLOCK, key_len), 1), jnp.int32(BLOCK))
        allowed = (jnp.abs(key_block - block) <= 1) | (key_block == 0)
        for choice in range(rand.shape[1]):
            allowed = allowed | (key_block == rand[block, choice])
        scores = dot(query[0, span, :], kvbuf[0].reshape(key_len, head), ((1,), (1,))) * scale
        unnorm = jnp.where(allowed, jnp.exp(scores), F32(0.0))
        prob[span, :] = unnorm / jnp.sum(unnorm, axis=1, keepdims=True)
    loop(blocks_here, probabilities)

    def terms(half, other):
        def body(owner):
            cols = pl.ds(pl.multiple_of(owner * n_tok, n_tok), n_tok)
            terms_out[half, owner] = dot(
                prob[:, cols].astype(BF16), other[0], ((0,), (0,))
            ).astype(BF16)

        loop(seq_count, body)

    terms(1, grad)
    terms_share(1)

    for at in range(1, count):
        gather_chunk(1, at)
    kv_share(1)

    def product(half, owner, span):
        src = pl.ds(pl.multiple_of(owner * rows + span.start, 128), TILE)
        return dot(turned[src, :], kv_grad[half], ((1,), (0,)))

    def chunk(at):
        return pl.ds(pl.multiple_of(at * part, 128), part)

    def to_sib(half, at, step):
        owner = peer_sib(step)

        def body(span):
            sib_out[half, step, span] = product(half, owner, span).astype(BF16)

        tile_loop(at * part, tiles, body)
        send(sib_out.at[half, step, chunk(at)], sib_in.at[half, step, chunk(at)],
             sib_send.at[half, step, at], sib_recv.at[half, step, at], {"seq": sib})

    def sib_arrived(half, at, step):
        arrived(sib_in.at[half, step, chunk(at)], sib_send.at[half, step, at],
                sib_recv.at[half, step, at])

    def to_peer(half, at, step):
        owner = peer(step)
        sib_arrived(half, at, step)

        def body(span):
            total = product(half, owner, span) + sib_in[half, step, span].astype(F32)
            peer_out[half, step, span] = total.astype(BF16)

        tile_loop(at * part, tiles, body)
        send(peer_out.at[half, step, chunk(at)], peer_in.at[half, step, chunk(at)],
             peer_send.at[half, step, at], peer_recv.at[half, step, at], {"seq": owner})

    def reduce_first(half):
        for step in range(1, chips):
            loop(count, lambda at: to_sib(half, at, step))
        for step in range(1, chips):
            to_peer(half, 0, step)

    def reduce_rest(half):
        for at in range(1, count):
            for step in range(1, chips):
                to_peer(half, at, step)
        loop(count, lambda at: to_sib(half, at, 0))

    def gossip_send(src, half, at, slot, partner):
        send(src.at[half, chunk(at)], gossip_in.at[slot, half, chunk(at)],
             gos_send.at[slot, half, at], gos_recv.at[slot, half, at], {"rep": partner})

    def gossip_arrived(half, at, slot):
        arrived(gossip_in.at[slot, half, chunk(at)], gos_send.at[slot, half, at],
                gos_recv.at[slot, half, at])

    def cols_of(half):
        return pl.ds(pl.multiple_of(half * head, 128), head)

    def reduce_end(half, at):
        sib_arrived(half, at, 0)
        for step in range(1, chips):
            arrived(peer_in.at[half, step, chunk(at)], peer_send.at[half, step, at],
                    peer_recv.at[half, step, at])

        def body(span):
            total = product(half, me, span) + sib_in[half, 0, span].astype(F32)
            for step in range(1, chips):
                total += peer_in[half, step, span].astype(F32)
            mixed[0, span, cols_of(half)] = total
            if dist:
                gossip_out[half, span] = total.astype(BF16)

        tile_loop(at * part, tiles, body)
        if dist:
            for slot in range(1 if two_step else len(partners)):
                gossip_send(gossip_out, half, at, slot, partners[slot])

    def gossip_relay(half, at):
        if two_step:
            gossip_arrived(half, at, 0)

            def body(span):
                total = mixed[0, span, cols_of(half)] + gossip_in[0, half, span].astype(F32)
                relay_out[half, span] = total.astype(BF16)

            tile_loop(at * part, tiles, body)
            gossip_send(relay_out, half, at, 1, pair_rep)

    def gossip_end(half, at):
        slots = [] if dist == 0 else [1] if two_step else list(range(len(partners)))
        for slot in slots:
            gossip_arrived(half, at, slot)

        def body(span):
            own = mixed[0, span, cols_of(half)]
            if dist == 0:
                total = own + own + own
            elif two_step:
                total = own + gossip_in[1, half, span].astype(F32)
            elif len(partners) == 1:
                other = gossip_in[0, half, span].astype(F32)
                total = own + other + other
            else:
                total = own + gossip_in[0, half, span].astype(F32)
                total += gossip_in[1, half, span].astype(F32)
            mixed[0, span, cols_of(half)] = total / F32(3.0)

        tile_loop(at * part, tiles, body)

    terms_collect(1)
    reduce_first(1)
    if dist:
        reduce_rest(1)

    kv_collect(1)
    def score_grads(blk):
        span = pl.ds(pl.multiple_of(blk * BLOCK, BLOCK), BLOCK)
        values = kvbuf[1].reshape(key_len, head)
        keys = kvbuf[0].reshape(key_len, head)
        prob_rows = prob[span, :]
        grad_rows = grad[0, span, :]
        context = dot(prob_rows.astype(BF16), values, ((1,), (0,)))
        delta = jnp.sum(grad_rows.astype(F32) * context, axis=1, keepdims=True)
        prob_grad = dot(grad_rows, values, ((1,), (1,)))
        score_grad = prob_rows * (prob_grad - delta) * scale
        prob[span, :] = score_grad
        query_grad[0, span, :] = dot(score_grad.astype(BF16), keys, ((1,), (0,))).astype(BF16)
    loop(blocks_here, score_grads)
    terms(0, query)
    terms_share(0)

    if dist:
        loop(count, lambda at: reduce_end(1, at))
    else:
        reduce_rest(1)
    terms_collect(0)
    reduce_first(0)
    if dist == 0:
        loop(count, lambda at: reduce_end(1, at))
    gossip_relay(1, 0)
    reduce_rest(0)
    for at in range(1, count):
        gossip_relay(1, at)
    loop(count, lambda at: reduce_end(0, at))
    loop(count, lambda at: gossip_relay(0, at))
    loop(2 * count, lambda item: gossip_end(1 - item // count, item % count))

    def drain(half):
        def drain_chunk(at):
            rows_at = w_rows(half, me, at)
            for step in range(chips):
                left(rows_at, w_send.at[half, step, at], w_recv.at[half, step, at])
                left(rows_at, sib_send.at[half, step, at], sib_recv.at[half, step, at])
            for step in range(1, chips):
                left(rows_at, fwd_send.at[half, step, at], fwd_recv.at[half, step, at])
                left(rows_at, peer_send.at[half, step, at], peer_recv.at[half, step, at])
            for slot in range(0 if dist == 0 else 2 if two_step else len(partners)):
                left(rows_at, gos_send.at[slot, half, at], gos_recv.at[slot, half, at])

        loop(count, drain_chunk)
        own = kvbuf.at[half, me]
        for step in range(chips):
            left(own, kv_send.at[half, step], kv_recv.at[half, step])
            left(own, term_send.at[half, step], term_recv.at[half, step])
        for step in range(1, chips):
            left(own, kv_fwd_send.at[half, step], kv_fwd_recv.at[half, step])
            left(own, sum_send.at[half, step], sum_recv.at[half, step])

    loop(2, drain)


def fused(tokens, queries, ctx_grad, kv_weight, rand_blocks, dist, ident):
    seq_count = lax.axis_size("seq")
    rep_count = lax.axis_size("rep")
    _, n_tok, width = tokens.shape
    _, rows, kv_width = kv_weight.shape
    head = kv_width // 2
    chips = seq_count // 2
    count = chunks_of(rows)
    dma = pltpu.SemaphoreType.DMA
    vmem = pl.BlockSpec(memory_space=pltpu.VMEM)
    anywhere = pl.BlockSpec(memory_space=pl.ANY)
    per_chip = dma((2, chips, count))
    per_pair = dma((2, chips))
    return pl.pallas_call(
        partial(kernel, dist, rep_count, seq_count),
        out_shape=(
            jax.ShapeDtypeStruct((1, rows, kv_width), F32),
            jax.ShapeDtypeStruct(queries.shape, BF16),
        ),
        in_specs=[anywhere, vmem, vmem, anywhere, pl.BlockSpec(memory_space=pltpu.SMEM)],
        out_specs=(vmem, vmem),
        scratch_shapes=[
            pltpu.VMEM((n_tok, width), BF16),
            pltpu.VMEM((width, n_tok), BF16),
            pltpu.VMEM((2, seq_count, rows, head), BF16),
            pltpu.VMEM((2, seq_count, n_tok, head), BF16),
            pltpu.VMEM((n_tok, seq_count * n_tok), F32),
            pltpu.VMEM((2, seq_count, n_tok, head), BF16),
            pltpu.VMEM((2, chips, n_tok, head), BF16),
            pltpu.VMEM((2, chips, n_tok, head), BF16),
            pltpu.VMEM((2, chips, n_tok, head), BF16),
            pltpu.VMEM((2, n_tok, head), BF16),
            pltpu.VMEM((n_tok, head), F32),
            pltpu.VMEM((2, chips, rows, head), BF16),
            pltpu.VMEM((2, chips, rows, head), BF16),
            pltpu.VMEM((2, chips, rows, head), BF16),
            pltpu.VMEM((2, chips, rows, head), BF16),
            pltpu.VMEM((2, rows, head), BF16),
            pltpu.VMEM((2, 2, rows, head), BF16),
            pltpu.VMEM((2, rows, head), BF16),
            dma((3,)),
            per_chip, per_chip, per_chip, per_chip,
            per_pair, per_pair, per_pair, per_pair,
            per_pair, per_pair, per_pair, per_pair,
            per_chip, per_chip, per_chip, per_chip,
            dma((2, 2, count)), dma((2, 2, count)),
        ],
        compiler_params=pltpu.CompilerParams(
            collective_id=ident, has_side_effects=True, vmem_limit_bytes=48 * 1024 * 1024
        ),
    )(tokens, queries, ctx_grad, kv_weight, rand_blocks)


def per_device(tokens, queries, ctx_grad, kv_weight, rand_blocks, step_count):
    rep_count = lax.axis_size("rep")
    branches = [
        partial(fused, dist=(1 << level) % rep_count, ident=level) for level in range(4)
    ]
    return lax.switch(
        step_count[0] % 4, branches, tokens, queries, ctx_grad, kv_weight, rand_blocks
    )


def solution(mesh):
    return jax.shard_map(
        per_device,
        mesh=mesh,
        in_specs=(
            P("rep", "seq", None),
            P("rep", "seq", None),
            P("rep", "seq", None),
            P("rep", "seq", None),
            P(),
            P(),
        ),
        out_specs=(P("rep", "seq", None), P("rep", "seq", None)),
        check_vma=False,
    )
```
